256 devices in a mesh: dp: 4 (over y), depth: 4 (over x), grid: 16 (over z, core).
Axes of the slice: x: 4, y: 4, z: 8, core: 2. Of those that a mesh axis runs over, the one named last changes fastest.
Arguments:
- tokens: bfloat16 [1024, 12288], P(('dp', 'depth'), 'grid'), may hold values from -6 to 6
- weight: bfloat16 [12288, 24576], P('grid', 'depth'), may hold values from -0.0546875 to 0.0546875
- cotangent: bfloat16 [1024, 24576], P(('dp', 'grid'), 'depth'), may hold values from -0.5 to 0.5
Outputs:
- hidden: bfloat16 [1024, 24576], P(('dp', 'grid'), 'depth')
- weight_grad: bfloat16 [12288, 24576], P(('grid', 'dp'), 'depth')
The draws below stay inside these ranges and needn't reach their ends.
All inputs are finite; a program needn't handle non-finite values.
Results may differ from the reference program's by a relative error of at most 0.011.
Values may be sent and summed in bfloat16 or wider, within the bound.
A program may use at most 64 MiB of HBM per device.

```python
import jax
import jax.numpy as jnp

D = 12288
FF = 24576
TOKENS = 1024


def level_of(key, dims, split, least, largest):
    def one(axis_at, shards_of):
        draws = jax.random.uniform(jax.random.fold_in(jax.random.fold_in(key, 6), axis_at), (shards_of,), jnp.float32, least / len(split), largest / len(split))
        return jnp.repeat(jnp.exp(draws), dims[axis_at] // shards_of).reshape((-1,) + (1,) * (len(dims) - axis_at - 1))

    loudness = one(*split[0])
    for cut in split[1:]:
        loudness = loudness * one(*cut)
    return loudness


def noise(own_key, shape, width, reach, split=(), kind=jnp.bfloat16):
    gain = level_of(own_key, shape, split, -0.22, 0.18) if split else 1.0
    result = jax.random.normal(own_key, shape, jnp.float32) * width * gain
    return jnp.minimum(jnp.maximum(result, -reach), reach).astype(kind)


def setup_inputs(seed: int = 0) -> dict:
    splits = jax.random.split(jax.random.key(seed), 4)
    tokens = noise(splits[0], (TOKENS, D), 1.0, 6.0, ((0, 16), (1, 16)))
    weight = noise(splits[1], (D, FF), D ** -0.5, 0.0546875, ((0, 16), (1, 4)))
    cotangent = noise(splits[2], (TOKENS, FF), (TOKENS ** -0.5), 0.5, ((0, 64), (1, 4)))
    return {"tokens": tokens, "weight": weight, "cotangent": cotangent}


def gelu_tanh(values):
    return jax.nn.gelu(values, approximate=True)

def reference(tokens, weight, cotangent):
    preact = jnp.dot(tokens, weight, preferred_element_type=jnp.float32)
    activated, pullback = jax.vjp(gelu_tanh, preact)
    grad_pre = pullback(cotangent.astype(jnp.float32))[0].astype(jnp.bfloat16)
    weight_grad = jnp.dot(tokens.T, grad_pre, preferred_element_type=jnp.float32)
    return (activated.astype(jnp.bfloat16), weight_grad.astype(jnp.bfloat16))
```

```python
import jax
import jax.numpy as jnp
from jax import lax
from jax.experimental import pallas as pl
from jax.experimental.pallas import tpu as pltpu
from jax.sharding import PartitionSpec as P

MESH = pl.DeviceIdType.MESH
F32, BF16 = jnp.float32, jnp.bfloat16
NY, NX, NZ = 4, 4, 8
N = 6
CW = 256
QUARTER = N * CW
KD = 768
ROWS = 16
OWN = 192
C1 = 0.7978845608028654
C2 = 0.044715


def remote(src, dst, sems, index, device):
    send, recv = sems
    return pltpu.make_async_remote_copy(
        src_ref=src, dst_ref=dst, send_sem=send.at[index], recv_sem=recv.at[index],
        device_id=device, device_id_type=MESH,
    )


def kernel(
    tok, wt, cot, hid, out,
    T, TT, Wv, Pf, Pb, Rc, S32, SB, R1, R2, G, GS, C, H, WG,
    tx_s, tx_r, ty_s, ty_r, tf_s, tf_r, pc_s, pc_r, rs_s, rs_r, yt_s, yt_r, ag_s, ag_r,
    gc_s, gc_r, wo_s, wo_r, w_sem, l_sem, o_sem,
):
    y, x, g = lax.axis_index("dp"), lax.axis_index("depth"), lax.axis_index("grid")
    z, c = g // 2, g % 2
    d = 1 - 2 * c

    def zmod(k):
        return (z + k + NZ) % NZ

    def at_z(k):
        return (y, x, zmod(k) * 2 + c)

    def at_x(k):
        return (y, (x + k) % NX, g)

    def at_y(k):
        return ((y + k) % NY, x, g)

    other = (y, x, z * 2 + 1 - c)

    own_tok = T.at[y, pl.ds(x * 4, 4)]
    tok_copy = pltpu.make_async_copy(tok, own_tok, l_sem.at[0])
    tok_copy.start()

    def w_copy(j, q):
        columns = pl.ds(pl.multiple_of(q * QUARTER + j * CW, CW), CW)
        return pltpu.make_async_copy(wt.at[:, columns], Wv.at[j, q], w_sem.at[j, q])

    for q in range(NY):
        w_copy(0, q).start()
    cot_copy = pltpu.make_async_copy(cot, C, l_sem.at[1])
    cot_copy.start()

    barrier = pltpu.get_barrier_semaphore()
    peers = [at_x(k) for k in (1, 2, 3)] + [at_y(k) for k in (1, 2, 3)]
    peers += [at_z(k) for k in (1, -1, 2, -2)] + [other]
    for peer in peers:
        pl.semaphore_signal(barrier, inc=1, device_id=peer, device_id_type=MESH)
    tok_copy.wait()
    pl.semaphore_wait(barrier, len(peers))

    def tok_x(k):
        return remote(own_tok, own_tok, (tx_s, tx_r), k - 1, at_x(k))

    def tok_x_in(k):
        here = T.at[y, pl.ds((x + NX - k) % NX * 4, 4)]
        return remote(here, here, (tx_s, tx_r), k - 1, at_x(k))

    def tok_y(k):
        return remote(own_tok, own_tok, (ty_s, ty_r), k - 1, at_y(k))

    def tok_y_in(k):
        here = T.at[(y + NY - k) % NY, pl.ds(x * 4, 4)]
        return remote(here, here, (ty_s, ty_r), k - 1, at_y(k))

    def tok_f(k, n):
        here = T.at[(y + NY - k) % NY, pl.ds(x * 4, 4)]
        return remote(here, here, (tf_s, tf_r), (k - 1, n - 1), at_x(n))

    def tok_f_in(k, n):
        here = T.at[(y + NY - k) % NY, pl.ds((x + NX - n) % NX * 4, 4)]
        return remote(here, here, (tf_s, tf_r), (k - 1, n - 1), at_x(n))

    for k in (2, 1, 3):
        tok_x(k).start()
    for k in (1, 3, 2):
        tok_y(k).start()

    @pl.loop(1, N)
    def _(j):
        for q in range(NY):
            w_copy(j, q).start()

    cot_copy.wait()
    for k in (1, 3, 2):
        tok_x_in(k).wait_recv()

    def pc(j):
        return remote(Pb.at[j, 1 - c], Rc.at[j], (pc_s, pc_r), j, other)

    def rs(j, n):
        sems = (rs_s, rs_r)
        if n == 0:
            return remote(SB.at[j, zmod(4)], R1.at[j, 0], sems, (j, 0), at_z(-2 * d))
        if n == 1:
            return remote(SB.at[j, zmod(-3 * d)], R1.at[j, 1], sems, (j, 1), at_z(-d))
        if n == 2:
            return remote(SB.at[j, zmod(3 * d)], R1.at[j, 2], sems, (j, 2), at_z(d))
        if n == 3:
            return remote(SB.at[j, zmod(-d)], R2.at[j, 0], sems, (j, 3), at_z(-d))
        if n == 4:
            return remote(SB.at[j, zmod(d)], R2.at[j, 1], sems, (j, 4), at_z(d))
        if n == 5:
            return remote(SB.at[j, zmod(-2 * d)], R2.at[j, 2], sems, (j, 5), at_z(-2 * d))
        return remote(SB.at[j, zmod(2 * d)], R2.at[j, 3], sems, (j, 6), at_z(2 * d))

    def yt(j, k):
        return remote(GS.at[j, (y + k) % NY], G.at[j, y, z, c], (yt_s, yt_r), (j, k - 1), at_y(k))

    def yt_in(j, k):
        here = G.at[j, (y + NY - k) % NY, z, c]
        return remote(here, here, (yt_s, yt_r), (j, k - 1), at_y(k))

    AG = ((0, 1), (0, -1), (0, 2), (0, -2), (-2, 1), (-2, 2), (2, -1))

    def ag(j, n):
        origin, to = AG[n]
        piece = G.at[j, :, zmod(origin * d), c]
        return remote(piece, piece, (ag_s, ag_r), (j, n), at_z(to * d))

    def ag_in(j, n):
        origin, to = AG[n]
        piece = G.at[j, :, zmod((origin - to) * d), c]
        return remote(piece, piece, (ag_s, ag_r), (j, n), at_z(to * d))

    def gc(j):
        piece = G.at[j, :, :, c]
        return remote(piece, piece, (gc_s, gc_r), j, other)

    def gc_in(j):
        piece = G.at[j, :, :, 1 - c]
        return remote(piece, piece, (gc_s, gc_r), j, other)

    def out_columns(group, j):
        return out.at[:, pl.ds(pl.multiple_of(group * QUARTER + j * CW, CW), CW)]

    def wo(j, k):
        return remote(WG.at[j, k], out_columns(y, j), (wo_s, wo_r), (j, k - 1), at_y(k))

    def wo_in(j, k):
        here = out_columns((y + NY - k) % NY, j)
        return remote(WG.at[j, k], here, (wo_s, wo_r), (j, k - 1), at_y(k))

    def wo_own(j):
        return pltpu.make_async_copy(WG.at[j, 0], out_columns(y, j), o_sem.at[j])

    def project(j):
        slot = j % 2
        rows = T[y].reshape(NZ * 2 * ROWS, KD)
        for q in range(NY):
            w_copy(j, q).wait()
            part = jnp.dot(rows, Wv[j, q], preferred_element_type=F32)
            part = part.reshape(NZ, 2, ROWS, CW)
            for core in range(2):
                Pf[slot, core, :, q] = part[:, core]
                Pb[j, core, :, q] = part[:, core].astype(BF16)
        pc(j).start()

    def reduce_first(j):
        pc(j).wait_recv()
        both = Pf[j % 2, c] + Rc[j].astype(F32)
        S32[j] = both
        SB[j] = both.astype(BF16)
        for n in (0, 1, 2, 3, 4):
            rs(j, n).start()

    def reduce_second(j):
        for n in (0, 1, 2):
            rs(j, n).wait_recv()
        near, far = zmod(-2 * d), zmod(2 * d)
        SB[j, near] = (S32[j, near] + R1[j, 0].astype(F32) + R1[j, 1].astype(F32)).astype(BF16)
        rs(j, 5).start()
        SB[j, far] = (S32[j, far] + R1[j, 2].astype(F32)).astype(BF16)
        rs(j, 6).start()

    def activate(j):
        for n in (3, 4, 5, 6):
            rs(j, n).wait_recv()
        v = S32[j, z] + R2[j, 0].astype(F32) + R2[j, 1].astype(F32)
        v = v + R2[j, 2].astype(F32) + R2[j, 3].astype(F32)
        square = v * v
        t = jnp.tanh(C1 * (v + C2 * (v * square)))
        half = 0.5 * (1.0 + t)
        slope = half + 0.5 * v * (1.0 - t * t) * (C1 * (1.0 + 3.0 * C2 * square))
        hidden = (v * half).astype(BF16)
        for q in range(NY):
            columns = pl.ds(pl.multiple_of(q * QUARTER + j * CW, CW), CW)
            H[:, columns] = hidden[q]
            GS[j, q] = (C[:, columns].astype(F32) * slope[q]).astype(BF16)
        for k in (2, 1, 3):
            yt(j, k).start()
        G[j, y, z, c] = GS[j, y]

    def gather_first(j):
        for k in (1, 3, 2):
            yt_in(j, k).wait_recv()
        for n in (2, 3, 0, 1):
            ag(j, n).start()

    def gather_second(j):
        ag_in(j, 2).wait_recv()
        ag(j, 5).start()
        ag(j, 4).start()
        ag_in(j, 3).wait_recv()
        ag(j, 6).start()

    def gather_cores(j):
        for n in (0, 1, 4, 5, 6):
            ag_in(j, n).wait_recv()
        gc(j).start()

    def weight_product(j):
        gc_in(j).wait_recv()
        for k in (2, 1, 3, 0):
            grad = G[j].reshape(NY * NZ * 2 * ROWS, CW)
            WG[j, k] = jnp.dot(TT[(y + k) % NY], grad, preferred_element_type=F32).astype(BF16)
            if k:
                wo(j, k).start()
            else:
                wo_own(j).start()

    def stage(j, run):
        pl.when(jnp.logical_and(j >= 0, j < N))(lambda: run(j))

    @pl.loop(-1, N + 5)
    def _(t):
        stage(t, reduce_first)

        @pl.when(t == 0)
        def _():
            for k in (1, 3, 2):
                tok_y_in(k).wait_recv()
                for n in (2, 1, 3):
                    tok_f(k, n).start()

        stage(t - 4, gather_second)
        stage(t - 1, reduce_second)
        stage(t - 3, gather_first)
        stage(t - 2, activate)
        stage(t - 5, gather_cores)
        stage(t + 1, project)

        @pl.when(jnp.logical_and(t >= 1, t <= 4))
        def _():
            k = t - 1

            @pl.when(k > 0)
            def _():
                for n in (1, 3, 2):
                    tok_f_in(k, n).wait_recv()

            group = (y + NY - k) % NY
            turned = T[group].reshape(NZ * 2 * ROWS, KD).T.reshape(NY, OWN, NZ * 2 * ROWS)
            TT[:, :, pl.ds(pl.multiple_of(group * 256, 256), 256)] = turned

        stage(t - 5, weight_product)

    hid_copy = pltpu.make_async_copy(H, hid, l_sem.at[2])
    hid_copy.start()
    for k in (1, 2, 3):
        tok_x(k).wait_send()
        tok_y(k).wait_send()
        for n in (1, 2, 3):
            tok_f(k, n).wait_send()

    @pl.loop(0, N)
    def _(j):
        pc(j).wait_send()
        gc(j).wait_send()
        for n in range(7):
            rs(j, n).wait_send()
            ag(j, n).wait_send()
        for k in (1, 2, 3):
            yt(j, k).wait_send()
            wo(j, k).wait_send()
            wo_in(j, k).wait_recv()
        wo_own(j).wait()

    hid_copy.wait()


def local(tokens, weight, cotangent):
    dma = pltpu.SemaphoreType.DMA
    piece = (NY, ROWS, CW)
    any_ref = pl.BlockSpec(memory_space=pl.ANY)
    pair = lambda *shape: [dma(shape), dma(shape)]
    hidden, grad = pl.pallas_call(
        kernel,
        out_shape=[
            jax.ShapeDtypeStruct(cotangent.shape, BF16),
            jax.ShapeDtypeStruct((OWN, weight.shape[1]), BF16),
        ],
        in_specs=[any_ref] * 3,
        out_specs=[any_ref] * 2,
        scratch_shapes=[
            pltpu.VMEM((NY, NZ * 2, ROWS, KD), BF16),
            pltpu.VMEM((NY, OWN, 1024), BF16),
            pltpu.VMEM((N, NY, KD, CW), BF16),
            pltpu.VMEM((2, 2, NZ) + piece, F32),
            pltpu.VMEM((N, 2, NZ) + piece, BF16),
            pltpu.VMEM((N, NZ) + piece, BF16),
            pltpu.VMEM((N, NZ) + piece, F32),
            pltpu.VMEM((N, NZ) + piece, BF16),
            pltpu.VMEM((N, 3) + piece, BF16),
            pltpu.VMEM((N, 4) + piece, BF16),
            pltpu.VMEM((N, NY, NZ, 2, ROWS, CW), BF16),
            pltpu.VMEM((N,) + piece, BF16),
            pltpu.VMEM(cotangent.shape, BF16),
            pltpu.VMEM(cotangent.shape, BF16),
            pltpu.VMEM((N, NY, OWN, CW), BF16),
            *pair(3), *pair(3), *pair(3, 3), *pair(N), *pair(N, 7), *pair(N, 3), *pair(N, 7),
            *pair(N), *pair(N, 3), dma((N, NY)), dma((3,)), dma((N,)),
        ],
        compiler_params=pltpu.CompilerParams(
            collective_id=0, has_side_effects=True, vmem_limit_bytes=56 * 2**20
        ),
        cost_estimate=pl.CostEstimate(
            flops=4 * 256 * 768 * 6144, bytes_accessed=13 * 2**20, transcendentals=16 * 6144
        ),
    )(tokens.reshape(4, ROWS, KD), weight, cotangent)
    return hidden, grad


def solution(mesh):
    return jax.shard_map(
        local,
        mesh=mesh,
        in_specs=(P(("dp", "depth"), "grid"), P("grid", "depth"), P(("dp", "grid"), "depth")),
        out_specs=(P(("dp", "grid"), "depth"), P(("grid", "dp"), "depth")),
        check_vma=False,
    )
```

```python
import jax
import jax.numpy as jnp
from jax import lax
from jax.experimental import pallas as pl
from jax.experimental.pallas import tpu as pltpu
from jax.sharding import PartitionSpec as P

MESH = pl.DeviceIdType.MESH
F32, BF16 = jnp.float32, jnp.bfloat16
NY, NX, NZ = 4, 4, 8
N = 12
CW = 128
AT = {"project": -5, "reduce_first": -4, "reduce_second": -1, "activate": 2, "gather_first": 4, "gather_second": 6, "gather_cores": 7, "weight_product": 8}
ORDER = ["activate", "turn", "forward", "gather_second", "gather_first", "reduce_second", "weight_product", "project", "gather_cores", "reduce_first"]
FORWARD = -3
TURN = (0, 2, 5, 6)
QUARTER = N * CW
KD = 768
ROWS = 16
OWN = 192
C1 = 0.7978845608028654
C2 = 0.044715


def remote(src, dst, sems, index, device):
    send, recv = sems
    return pltpu.make_async_remote_copy(
        src_ref=src, dst_ref=dst, send_sem=send.at[index], recv_sem=recv.at[index],
        device_id=device, device_id_type=MESH,
    )


def kernel(
    tok, wt, cot, hid, out,
    T, TT, Wv, Pf, Pb, Rc, S32, SB, R1, R2, G, GS, C, H, WG,
    tx_s, tx_r, ty_s, ty_r, tf_s, tf_r, pc_s, pc_r, rs_s, rs_r, yt_s, yt_r, ag_s, ag_r,
    gc_s, gc_r, wo_s, wo_r, w_sem, l_sem, o_sem,
):
    y, x, g = lax.axis_index("dp"), lax.axis_index("depth"), lax.axis_index("grid")
    z, c = g // 2, g % 2
    d = 1 - 2 * c

    def zmod(k):
        return (z + k + NZ) % NZ

    def at_z(k):
        return (y, x, zmod(k) * 2 + c)

    def at_x(k):
        return (y, (x + k) % NX, g)

    def at_y(k):
        return ((y + k) % NY, x, g)

    other = (y, x, z * 2 + 1 - c)

    barrier = pltpu.get_barrier_semaphore()
    peers = [at_x(2), at_y(2), at_z(2), at_z(-2), at_x(1), at_x(3), at_y(1), at_y(3), at_z(1), at_z(-1), other]
    for peer in peers:
        pl.semaphore_signal(barrier, inc=1, device_id=peer, device_id_type=MESH)

    own_tok = T.at[y, pl.ds(x * 4, 4)]
    tok_copy = pltpu.make_async_copy(tok, own_tok, l_sem.at[0])
    tok_copy.start()

    def w_copy(j, q):
        columns = pl.ds(pl.multiple_of(q * QUARTER + j * CW, CW), CW)
        return pltpu.make_async_copy(wt.at[:, columns], Wv.at[j, q], w_sem.at[j, q])

    for q in range(NY):
        w_copy(0, q).start()
    cot_copy = pltpu.make_async_copy(cot, C, l_sem.at[1])
    cot_copy.start()

    tok_copy.wait()
    pl.semaphore_wait(barrier, len(peers))

    def tok_x(k):
        return remote(own_tok, own_tok, (tx_s, tx_r), k - 1, at_x(k))

    def tok_x_in(k):
        here = T.at[y, pl.ds((x + NX - k) % NX * 4, 4)]
        return remote(here, here, (tx_s, tx_r), k - 1, at_x(k))

    def tok_y(k):
        return remote(own_tok, own_tok, (ty_s, ty_r), k - 1, at_y(k))

    def tok_y_in(k):
        here = T.at[(y + NY - k) % NY, pl.ds(x * 4, 4)]
        return remote(here, here, (ty_s, ty_r), k - 1, at_y(k))

    def tok_f(k, n):
        here = T.at[(y + NY - k) % NY, pl.ds(x * 4, 4)]
        return remote(here, here, (tf_s, tf_r), (k - 1, n - 1), at_x(n))

    def tok_f_in(k, n):
        here = T.at[(y + NY - k) % NY, pl.ds((x + NX - n) % NX * 4, 4)]
        return remote(here, here, (tf_s, tf_r), (k - 1, n - 1), at_x(n))

    for k in (2, 1, 3):
        tok_x(k).start()
    for k in (1, 3, 2):
        tok_y(k).start()

    @pl.loop(1, N)
    def _(j):
        for q in range(NY):
            w_copy(j, q).start()

    cot_copy.wait()
    for k in (1, 3, 2):
        tok_x_in(k).wait_recv()

    def pc(j):
        return remote(Pb.at[j, 1 - c], Rc.at[j], (pc_s, pc_r), j, other)

    def rs(j, n):
        sems = (rs_s, rs_r)
        if n == 0:
            return remote(SB.at[j, zmod(4)], R1.at[j, 0], sems, (j, 0), at_z(-2 * d))
        if n == 1:
            return remote(SB.at[j, zmod(-3 * d)], R1.at[j, 1], sems, (j, 1), at_z(-d))
        if n == 2:
            return remote(SB.at[j, zmod(3 * d)], R1.at[j, 2], sems, (j, 2), at_z(d))
        if n == 3:
            return remote(SB.at[j, zmod(-d)], R2.at[j, 0], sems, (j, 3), at_z(-d))
        if n == 4:
            return remote(SB.at[j, zmod(d)], R2.at[j, 1], sems, (j, 4), at_z(d))
        if n == 5:
            return remote(SB.at[j, zmod(-2 * d)], R2.at[j, 2], sems, (j, 5), at_z(-2 * d))
        return remote(SB.at[j, zmod(2 * d)], R2.at[j, 3], sems, (j, 6), at_z(2 * d))

    def yt(j, k):
        return remote(GS.at[j, (y + k) % NY], G.at[j, y, z, c], (yt_s, yt_r), (j, k - 1), at_y(k))

    def yt_in(j, k):
        here = G.at[j, (y + NY - k) % NY, z, c]
        return remote(here, here, (yt_s, yt_r), (j, k - 1), at_y(k))

    AG = ((0, 1), (0, -1), (0, 2), (0, -2), (-2, 1), (-2, 2), (2, -1))

    def ag(j, n):
        origin, to = AG[n]
        piece = G.at[j, :, zmod(origin * d), c]
        return remote(piece, piece, (ag_s, ag_r), (j, n), at_z(to * d))

    def ag_in(j, n):
        origin, to = AG[n]
        piece = G.at[j, :, zmod((origin - to) * d), c]
        return remote(piece, piece, (ag_s, ag_r), (j, n), at_z(to * d))

    def gc(j):
        piece = G.at[j, :, :, c]
        return remote(piece, piece, (gc_s, gc_r), j, other)

    def gc_in(j):
        piece = G.at[j, :, :, 1 - c]
        return remote(piece, piece, (gc_s, gc_r), j, other)

    def out_columns(group, j):
        return out.at[:, pl.ds(pl.multiple_of(group * QUARTER + j * CW, CW), CW)]

    def wo(j, k):
        return remote(WG.at[j, k], out_columns(y, j), (wo_s, wo_r), (j, k - 1), at_y(k))

    def wo_in(j, k):
        here = out_columns((y + NY - k) % NY, j)
        return remote(WG.at[j, k], here, (wo_s, wo_r), (j, k - 1), at_y(k))

    def wo_own(j):
        return pltpu.make_async_copy(WG.at[j, 0], out_columns(y, j), o_sem.at[j])

    def project(j):
        slot = j % 3
        rows = T[y].reshape(NZ * 2 * ROWS, KD)
        for q in range(NY):
            w_copy(j, q).wait()
            part = jnp.dot(rows, Wv[j, q], preferred_element_type=F32)
            part = part.reshape(NZ, 2, ROWS, CW)
            for core in range(2):
                Pf[slot, core, :, q] = part[:, core]
                Pb[j, core, :, q] = part[:, core].astype(BF16)
        pc(j).start()

    def reduce_first(j):
        pc(j).wait_recv()
        both = Pf[j % 3, c] + Rc[j].astype(F32)
        S32[j] = both
        SB[j] = both.astype(BF16)
        for n in (0, 1, 2, 3, 4):
            rs(j, n).start()

    def reduce_second(j):
        for n in (0, 1, 2):
            rs(j, n).wait_recv()
        near, far = zmod(-2 * d), zmod(2 * d)
        SB[j, near] = (S32[j, near] + R1[j, 0].astype(F32) + R1[j, 1].astype(F32)).astype(BF16)
        rs(j, 5).start()
        SB[j, far] = (S32[j, far] + R1[j, 2].astype(F32)).astype(BF16)
        rs(j, 6).start()

    def activate(j):
        for n in (3, 4, 5, 6):
            rs(j, n).wait_recv()
        v = S32[j, z] + R2[j, 0].astype(F32) + R2[j, 1].astype(F32)
        v = v + R2[j, 2].astype(F32) + R2[j, 3].astype(F32)
        square = v * v
        t = jnp.tanh(C1 * (v + C2 * (v * square)))
        half = 0.5 * (1.0 + t)
        slope = half + 0.5 * v * (1.0 - t * t) * (C1 * (1.0 + 3.0 * C2 * square))
        hidden = (v * half).astype(BF16)
        for q in range(NY):
            columns = pl.ds(pl.multiple_of(q * QUARTER + j * CW, CW), CW)
            H[:, columns] = hidden[q]
            GS[j, q] = (C[:, columns].astype(F32) * slope[q]).astype(BF16)
        for k in (2, 1, 3):
            yt(j, k).start()
        G[j, y, z, c] = GS[j, y]

    def gather_first(j):
        for k in (1, 3, 2):
            yt_in(j, k).wait_recv()
        for n in (2, 3, 0, 1):
            ag(j, n).start()

    def gather_second(j):
        ag_in(j, 2).wait_recv()
        ag(j, 5).start()
        ag(j, 4).start()
        ag_in(j, 3).wait_recv()
        ag(j, 6).start()

    def gather_cores(j):
        for n in (0, 1, 4, 5, 6):
            ag_in(j, n).wait_recv()
        gc(j).start()

    def weight_product(j):
        gc_in(j).wait_recv()
        for k in (2, 1, 3, 0):
            grad = G[j].reshape(NY * NZ * 2 * ROWS, CW)
            WG[j, k] = jnp.dot(TT[(y + k) % NY], grad, preferred_element_type=F32).astype(BF16)
            if k:
                wo(j, k).start()
            else:
                wo_own(j).start()

    def retire(j):
        pc(j).wait_send()
        gc(j).wait_send()
        for n in range(7):
            rs(j, n).wait_send()
            ag(j, n).wait_send()
        for k in (1, 2, 3):
            yt(j, k).wait_send()

    def forward(t):
        for k in (1, 3, 2):
            tok_y_in(k).wait_recv()
            for n in (2, 1, 3):
                tok_f(k, n).start()

    def turn(t):
        def run(k):
            if k:
                for n in (1, 3, 2):
                    tok_f_in(k, n).wait_recv()
            group = (y + NY - k) % NY
            turned = T[group].reshape(NZ * 2 * ROWS, KD).T.reshape(NY, OWN, NZ * 2 * ROWS)
            TT[:, :, pl.ds(pl.multiple_of(group * 256, 256), 256)] = turned

        for k in range(NY):
            pl.when(t == TURN[k])(lambda k=k: run(k))

    stages = {
        "project": project, "reduce_first": reduce_first, "reduce_second": reduce_second,
        "activate": activate, "gather_first": gather_first, "gather_second": gather_second,
        "gather_cores": gather_cores, "weight_product": weight_product, "retire": retire,
    }

    at = dict(AT, retire=AT["weight_product"] + 1)

    @pl.loop(min(AT.values()), N + AT["weight_product"])
    def _(t):
        for name in ORDER + ["retire"]:
            if name == "forward":
                pl.when(t == FORWARD)(lambda: forward(t))
            elif name == "turn":
                turn(t)
            else:
                j = t - at[name]
                pl.when(jnp.logical_and(j >= 0, j < N))(lambda run=stages[name], j=j: run(j))

    hid_copy = pltpu.make_async_copy(H, hid, l_sem.at[2])
    hid_copy.start()
    for k in (1, 2, 3):
        tok_x(k).wait_send()
        tok_y(k).wait_send()
        for n in (1, 2, 3):
            tok_f(k, n).wait_send()

    retire(N - 1)

    @pl.loop(0, N)
    def _(j):
        for k in (1, 2, 3):
            wo(j, k).wait_send()
            wo_in(j, k).wait_recv()
        wo_own(j).wait()

    hid_copy.wait()


def place(hidden, grad, hidden_out, grad_out, H, W, sem_in, sem_out):
    parts = [(hidden, H, hidden_out)]
    for n in range(6):
        rows = pl.ds(n * 32, 32)
        parts.append((grad.at[rows], W.at[rows], grad_out.at[rows]))
    come = [pltpu.make_async_copy(p[0], p[1], sem_in.at[n]) for n, p in enumerate(parts)]
    go = [pltpu.make_async_copy(p[1], p[2], sem_out.at[n]) for n, p in enumerate(parts)]
    for copy in come:
        copy.start()
    for one, two in zip(come, go):
        one.wait()
        two.start()
    for copy in go:
        copy.wait()


def local(tokens, weight, cotangent):
    dma = pltpu.SemaphoreType.DMA
    piece = (NY, ROWS, CW)
    any_ref = pl.BlockSpec(memory_space=pl.ANY)
    pair = lambda *shape: [dma(shape), dma(shape)]
    hidden, grad = pl.pallas_call(
        kernel,
        out_shape=[
            jax.ShapeDtypeStruct(cotangent.shape, BF16),
            jax.ShapeDtypeStruct((OWN, weight.shape[1]), BF16),
        ],
        in_specs=[pl.BlockSpec(memory_space=pltpu.HBM)] * 3,
        out_specs=[any_ref] * 2,
        scratch_shapes=[
            pltpu.VMEM((NY, NZ * 2, ROWS, KD), BF16),
            pltpu.VMEM((NY, OWN, 1024), BF16),
            pltpu.VMEM((N, NY, KD, CW), BF16),
            pltpu.VMEM((3, 2, NZ) + piece, F32),
            pltpu.VMEM((N, 2, NZ) + piece, BF16),
            pltpu.VMEM((N, NZ) + piece, BF16),
            pltpu.VMEM((N, NZ) + piece, F32),
            pltpu.VMEM((N, NZ) + piece, BF16),
            pltpu.VMEM((N, 3) + piece, BF16),
            pltpu.VMEM((N, 4) + piece, BF16),
            pltpu.VMEM((N, NY, NZ, 2, ROWS, CW), BF16),
            pltpu.VMEM((N,) + piece, BF16),
            pltpu.VMEM(cotangent.shape, BF16),
            pltpu.VMEM(cotangent.shape, BF16),
            pltpu.VMEM((N, NY, OWN, CW), BF16),
            *pair(3), *pair(3), *pair(3, 3), *pair(N), *pair(N, 7), *pair(N, 3), *pair(N, 7),
            *pair(N), *pair(N, 3), dma((N, NY)), dma((3,)), dma((N,)),
        ],
        compiler_params=pltpu.CompilerParams(
            collective_id=0, has_side_effects=True, vmem_limit_bytes=51 * 2**20
        ),
        cost_estimate=pl.CostEstimate(
            flops=4 * 256 * 768 * 6144, bytes_accessed=13 * 2**20, transcendentals=16 * 6144
        ),
    )(*[pltpu.with_memory_space_constraint(a, pltpu.HBM) for a in (tokens.reshape(4, ROWS, KD), weight, cotangent)])
    return hidden, grad


def solution(mesh):
    return jax.shard_map(
        local,
        mesh=mesh,
        in_specs=(P(("dp", "depth"), "grid"), P("grid", "depth"), P(("dp", "grid"), "depth")),
        out_specs=(P(("dp", "grid"), "depth"), P(("grid", "dp"), "depth")),
        check_vma=False,
    )
```

```python
import jax
import jax.numpy as jnp
from jax import lax
from jax.experimental import pallas as pl
from jax.experimental.pallas import tpu as pltpu
from jax.sharding import PartitionSpec as P

MESH = pl.DeviceIdType.MESH
F32, BF16 = jnp.float32, jnp.bfloat16
NY, NX, NZ = 4, 4, 8
N = 12
CW = 128
AT = {"project": -5, "reduce_first": -4, "reduce_second": -1, "activate": 2, "gather_first": 4, "gather_second": 6, "gather_cores": 7, "weight_product": 8}
ORDER = ["activate", "turn", "forward", "gather_second", "gather_first", "reduce_second", "weight_product", "project", "gather_cores", "reduce_first"]
FORWARD = -3
TURN = (0, 2, 5, 6)
QUARTER = N * CW
KD = 768
ROWS = 16
OWN = 192
C1 = 0.7978845608028654
C2 = 0.044715


TX, TY, TF, PC, RS, YT, AGS, GC, WO = range(9)


def kernel(
    tok, wt, cot, hid, out,
    T, TT, Wv, Pf, Pb, Rc, S32, SB, R1, R2, G, GS, C, H, WG,
    send, tx_r, ty_r, tf_r, pc_r, ra_r, rb_r, yt_r, ag_r, gc_r, wo_r, w_sem, l_sem, o_sem,
):
    y, x, g = lax.axis_index("dp"), lax.axis_index("depth"), lax.axis_index("grid")
    z, c = g // 2, g % 2
    d = 1 - 2 * c

    def zmod(k):
        return (z + k + NZ) % NZ

    def at_z(k):
        return (y, x, zmod(k) * 2 + c)

    def at_x(k):
        return (y, (x + k) % NX, g)

    def at_y(k):
        return ((y + k) % NY, x, g)

    other = (y, x, z * 2 + 1 - c)

    def remote(src, dst, kind, recv, device):
        return pltpu.make_async_remote_copy(
            src_ref=src, dst_ref=dst, send_sem=send.at[kind], recv_sem=recv,
            device_id=device, device_id_type=MESH,
        )

    def arrived(like, recv):
        remote(like, like, 0, recv, other).wait_recv()

    def sent(like, kind):
        remote(like, like, kind, tx_r.at[0], other).wait_send()

    barrier = pltpu.get_barrier_semaphore()
    peers = [at_x(2), at_y(2), at_z(2), at_z(-2), at_x(1), at_x(3), at_y(1), at_y(3), at_z(1), at_z(-1), other]
    for peer in peers:
        pl.semaphore_signal(barrier, inc=1, device_id=peer, device_id_type=MESH)

    own_tok = T.at[y, pl.ds(x * 4, 4)]
    tok_copy = pltpu.make_async_copy(tok, own_tok, l_sem.at[0])
    tok_copy.start()

    def w_copy(j, q):
        columns = pl.ds(pl.multiple_of(q * QUARTER + j * CW, CW), CW)
        return pltpu.make_async_copy(wt.at[:, columns], Wv.at[j, q], w_sem.at[j])

    for q in range(NY):
        w_copy(0, q).start()
    cot_copy = pltpu.make_async_copy(cot, C, l_sem.at[1])
    cot_copy.start()

    tok_copy.wait()
    pl.semaphore_wait(barrier, len(peers))

    def tok_x(k):
        return remote(own_tok, own_tok, TX, tx_r.at[0], at_x(k))

    def tok_y(k):
        return remote(own_tok, own_tok, TY, ty_r.at[k - 1], at_y(k))

    def tok_f(k, n):
        here = T.at[(y + NY - k) % NY, pl.ds(x * 4, 4)]
        return remote(here, here, TF, tf_r.at[k - 1], at_x(n))

    three = T.at[0, pl.ds(0, 12)]

    for k in (2, 1, 3):
        tok_x(k).start()
    for k in (1, 3, 2):
        tok_y(k).start()

    @pl.loop(1, N)
    def _(j):
        for q in range(NY):
            w_copy(j, q).start()

    cot_copy.wait()
    arrived(three, tx_r.at[0])

    def pc(j):
        return remote(Pb.at[j, 1 - c], Rc.at[j], PC, pc_r.at[j], other)

    SUMS = ((4, -2, 0), (-3, -1, 1), (3, 1, 2), (-1, -1, 3), (1, 1, 4), (-2, -2, 5), (2, 2, 6))

    def rs(j, n):
        owner, to, place = SUMS[n]
        here, recv = (R1.at[j, place], ra_r) if place < 3 else (R2.at[j, place - 3], rb_r)
        return remote(SB.at[j, zmod(owner * d)], here, RS, recv.at[j], at_z(to * d))

    def yt(j, k):
        return remote(GS.at[j, (y + k) % NY], G.at[j, y, z, c], YT, yt_r.at[j], at_y(k))

    AG = ((0, 1), (0, -1), (0, 2), (0, -2), (-2, 1), (-2, 2), (2, -1))

    def ag(j, n):
        origin, to = AG[n]
        piece = G.at[j, :, zmod(origin * d), c]
        recv = ag_r.at[j, {2: 0, 3: 1}.get(n, 2)]
        return remote(piece, piece, AGS, recv, at_z(to * d))

    def gc(j):
        piece = G.at[j, :, :, c]
        return remote(piece, piece, GC, gc_r.at[j], other)

    def out_columns(group, j):
        return out.at[:, pl.ds(pl.multiple_of(group * QUARTER + j * CW, CW), CW)]

    def wo(j, k):
        return remote(WG.at[j, k], out_columns(y, j), WO, wo_r.at[0], at_y(k))

    def wo_own(j):
        return pltpu.make_async_copy(WG.at[j, 0], out_columns(y, j), o_sem.at[0])

    def project(j):
        slot = j % 3
        rows = T[y].reshape(NZ * 2 * ROWS, KD)
        pltpu.make_async_copy(Wv.at[j], Wv.at[j], w_sem.at[j]).wait()
        for q in range(NY):
            part = jnp.dot(rows, Wv[j, q], preferred_element_type=F32)
            part = part.reshape(NZ, 2, ROWS, CW)
            for core in range(2):
                Pf[slot, core, :, q] = part[:, core]
                Pb[j, core, :, q] = part[:, core].astype(BF16)
        pc(j).start()

    def reduce_first(j):
        arrived(Rc.at[j], pc_r.at[j])
        both = Pf[j % 3, c] + Rc[j].astype(F32)
        S32[j] = both
        SB[j] = both.astype(BF16)
        for n in (0, 1, 2, 3, 4):
            rs(j, n).start()

    def reduce_second(j):
        arrived(R1.at[j], ra_r.at[j])
        near, far = zmod(-2 * d), zmod(2 * d)
        SB[j, near] = (S32[j, near] + R1[j, 0].astype(F32) + R1[j, 1].astype(F32)).astype(BF16)
        rs(j, 5).start()
        SB[j, far] = (S32[j, far] + R1[j, 2].astype(F32)).astype(BF16)
        rs(j, 6).start()

    def activate(j):
        arrived(R2.at[j], rb_r.at[j])
        v = S32[j, z] + R2[j, 0].astype(F32) + R2[j, 1].astype(F32)
        v = v + R2[j, 2].astype(F32) + R2[j, 3].astype(F32)
        square = v * v
        t = jnp.tanh(C1 * (v + C2 * (v * square)))
        half = 0.5 * (1.0 + t)
        slope = half + 0.5 * v * (1.0 - t * t) * (C1 * (1.0 + 3.0 * C2 * square))
        hidden = (v * half).astype(BF16)
        for q in range(NY):
            columns = pl.ds(pl.multiple_of(q * QUARTER + j * CW, CW), CW)
            H[:, columns] = hidden[q]
            GS[j, q] = (C[:, columns].astype(F32) * slope[q]).astype(BF16)
        for k in (2, 1, 3):
            yt(j, k).start()
        G[j, y, z, c] = GS[j, y]

    def gather_first(j):
        arrived(GS.at[j, pl.ds(0, 3)], yt_r.at[j])
        for n in (2, 3, 0, 1):
            ag(j, n).start()

    def gather_second(j):
        arrived(SB.at[j, 0], ag_r.at[j, 0])
        ag(j, 5).start()
        ag(j, 4).start()
        arrived(SB.at[j, 0], ag_r.at[j, 1])
        ag(j, 6).start()

    def gather_cores(j):
        arrived(SB.at[j, pl.ds(0, 5)], ag_r.at[j, 2])
        gc(j).start()

    def weight_product(j):
        arrived(G.at[j, :, :, 1 - c], gc_r.at[j])
        for k in (2, 1, 3, 0):
            grad = G[j].reshape(NY * NZ * 2 * ROWS, CW)
            WG[j, k] = jnp.dot(TT[(y + k) % NY], grad, preferred_element_type=F32).astype(BF16)
            if k:
                wo(j, k).start()
            else:
                wo_own(j).start()

    def forward(t):
        for k in (1, 3, 2):
            arrived(own_tok, ty_r.at[k - 1])
            for n in (2, 1, 3):
                tok_f(k, n).start()

    def turn(t):
        def run(k):
            if k:
                arrived(three, tf_r.at[k - 1])
            group = (y + NY - k) % NY
            turned = T[group].reshape(NZ * 2 * ROWS, KD).T.reshape(NY, OWN, NZ * 2 * ROWS)
            TT[:, :, pl.ds(pl.multiple_of(group * 256, 256), 256)] = turned

        for k in range(NY):
            pl.when(t == TURN[k])(lambda k=k: run(k))

    stages = {
        "project": project, "reduce_first": reduce_first, "reduce_second": reduce_second,
        "activate": activate, "gather_first": gather_first, "gather_second": gather_second,
        "gather_cores": gather_cores, "weight_product": weight_product,
    }

    @pl.loop(min(AT.values()), N + AT["weight_product"])
    def _(t):
        for name in ORDER:
            if name == "forward":
                pl.when(t == FORWARD)(lambda: forward(t))
            elif name == "turn":
                turn(t)
            else:
                j = t - AT[name]
                pl.when(jnp.logical_and(j >= 0, j < N))(lambda run=stages[name], j=j: run(j))

    hid_copy = pltpu.make_async_copy(H, hid, l_sem.at[2])
    hid_copy.start()
    sent(three, TX)
    sent(three, TY)
    sent(T.at[pl.ds(0, 3), pl.ds(0, 12)], TF)
    sent(Pb.at[:, 0], PC)
    sent(SB.at[:, pl.ds(0, 7)], RS)
    sent(GS.at[:, pl.ds(0, 3)], YT)
    sent(SB.at[:, pl.ds(0, 7)], AGS)
    sent(G.at[:, :, :, 0], GC)
    sent(WG.at[:, pl.ds(0, 3)], WO)
    arrived(WG.at[:, pl.ds(0, 3)], wo_r.at[0])
    pltpu.make_async_copy(WG.at[:, 0], WG.at[:, 0], o_sem.at[0]).wait()
    hid_copy.wait()


def place(hidden, grad, hidden_out, grad_out, H, W, sem_in, sem_out):
    parts = [(hidden, H, hidden_out)]
    for n in range(6):
        rows = pl.ds(n * 32, 32)
        parts.append((grad.at[rows], W.at[rows], grad_out.at[rows]))
    come = [pltpu.make_async_copy(p[0], p[1], sem_in.at[n]) for n, p in enumerate(parts)]
    go = [pltpu.make_async_copy(p[1], p[2], sem_out.at[n]) for n, p in enumerate(parts)]
    for copy in come:
        copy.start()
    for one, two in zip(come, go):
        one.wait()
        two.start()
    for copy in go:
        copy.wait()


def local(tokens, weight, cotangent):
    dma = pltpu.SemaphoreType.DMA
    piece = (NY, ROWS, CW)
    any_ref = pl.BlockSpec(memory_space=pl.ANY)
    hidden, grad = pl.pallas_call(
        kernel,
        out_shape=[
            jax.ShapeDtypeStruct(cotangent.shape, BF16),
            jax.ShapeDtypeStruct((OWN, weight.shape[1]), BF16),
        ],
        in_specs=[pl.BlockSpec(memory_space=pltpu.HBM)] * 3,
        out_specs=[any_ref] * 2,
        scratch_shapes=[
            pltpu.VMEM((NY, NZ * 2, ROWS, KD), BF16),
            pltpu.VMEM((NY, OWN, 1024), BF16),
            pltpu.VMEM((N, NY, KD, CW), BF16),
            pltpu.VMEM((3, 2, NZ) + piece, F32),
            pltpu.VMEM((N, 2, NZ) + piece, BF16),
            pltpu.VMEM((N, NZ) + piece, BF16),
            pltpu.VMEM((N, NZ) + piece, F32),
            pltpu.VMEM((N, NZ) + piece, BF16),
            pltpu.VMEM((N, 3) + piece, BF16),
            pltpu.VMEM((N, 4) + piece, BF16),
            pltpu.VMEM((N, NY, NZ, 2, ROWS, CW), BF16),
            pltpu.VMEM((N,) + piece, BF16),
            pltpu.VMEM(cotangent.shape, BF16),
            pltpu.VMEM(cotangent.shape, BF16),
            pltpu.VMEM((N, NY, OWN, CW), BF16),
            dma((9,)), dma((1,)), dma((3,)), dma((3,)), dma((N,)), dma((N,)), dma((N,)), dma((N,)),
            dma((N, 3)), dma((N,)), dma((1,)), dma((N,)), dma((3,)), dma((1,)),
        ],
        compiler_params=pltpu.CompilerParams(
            collective_id=0, has_side_effects=True, vmem_limit_bytes=51 * 2**20
        ),
        cost_estimate=pl.CostEstimate(
            flops=4 * 256 * 768 * 6144, bytes_accessed=13 * 2**20, transcendentals=16 * 6144
        ),
    )(*[pltpu.with_memory_space_constraint(a, pltpu.HBM) for a in (tokens.reshape(4, ROWS, KD), weight, cotangent)])
    return hidden, grad


def solution(mesh):
    return jax.shard_map(
        local,
        mesh=mesh,
        in_specs=(P(("dp", "depth"), "grid"), P("grid", "depth"), P(("dp", "grid"), "depth")),
        out_specs=(P(("dp", "grid"), "depth"), P(("grid", "dp"), "depth")),
        check_vma=False,
    )
```

```python
import jax
import jax.numpy as jnp
from jax import lax
from jax.experimental import pallas as pl
from jax.experimental.pallas import tpu as pltpu
from jax.sharding import PartitionSpec as P

MESH = pl.DeviceIdType.MESH
F32, BF16 = jnp.float32, jnp.bfloat16
NY, NX, NZ = 4, 4, 8
N = 12
CW = 128
AT = {"project": -5, "reduce_first": -4, "reduce_second": -1, "activate": 2, "gather_first": 4, "gather_second": 6, "gather_cores": 7, "weight_product": 8}
ORDER = ["activate", "turn", "forward", "gather_second", "gather_first", "reduce_second", "weight_product", "project", "gather_cores", "reduce_first"]
FORWARD = -3
TURN = (0, 2, 5, 6)
QUARTER = N * CW
KD = 768
ROWS = 16
OWN = 192
C1 = 0.7978845608028654
C2 = 0.044715


TX, TY, TF, PC, RS, YT, AGS, GC, WO = range(9)


def kernel(
    tok, wt, cot, hid, out,
    T, TT, Wv, Pf, Pb, Rc, S32, SB, R1, R2, G, GS, C, H, WG,
    send, tx_r, ty_r, tf_r, pc_r, ra_r, rb_r, yt_r, ag_r, gc_r, wo_r, w_sem, l_sem, o_sem,
):
    y, x, g = lax.axis_index("dp"), lax.axis_index("depth"), lax.axis_index("grid")
    z, c = g // 2, g % 2
    d = 1 - 2 * c

    def zmod(k):
        return (z + k + NZ) % NZ

    def at_z(k):
        return (y, x, zmod(k) * 2 + c)

    def at_x(k):
        return (y, (x + k) % NX, g)

    def at_y(k):
        return ((y + k) % NY, x, g)

    other = (y, x, z * 2 + 1 - c)

    def remote(src, dst, kind, recv, device):
        return pltpu.make_async_remote_copy(
            src_ref=src, dst_ref=dst, send_sem=send.at[kind], recv_sem=recv,
            device_id=device, device_id_type=MESH,
        )

    def arrived(like, recv):
        remote(like, like, 0, recv, other).wait_recv()

    def sent(like, kind):
        remote(like, like, kind, tx_r.at[0], other).wait_send()

    barrier = pltpu.get_barrier_semaphore()
    peers = [at_x(2), at_y(2), at_z(2), at_z(-2), at_x(1), at_x(3), at_y(1), at_y(3), at_z(1), at_z(-1), other]
    for peer in peers:
        pl.semaphore_signal(barrier, inc=1, device_id=peer, device_id_type=MESH)

    own_tok = T.at[y, pl.ds(x * 4, 4)]
    tok_copy = pltpu.make_async_copy(tok, own_tok, l_sem.at[0])
    tok_copy.start()

    def w_copy(j, q):
        columns = pl.ds(pl.multiple_of(q * QUARTER + j * CW, CW), CW)
        return pltpu.make_async_copy(wt.at[:, columns], Wv.at[j, q], w_sem.at[j])

    for q in range(NY):
        w_copy(0, q).start()
    cot_copy = pltpu.make_async_copy(cot, C, l_sem.at[1])
    cot_copy.start()

    tok_copy.wait()
    pl.semaphore_wait(barrier, len(peers))

    def tok_x(k):
        return remote(own_tok, own_tok, TX, tx_r.at[0], at_x(k))

    def tok_y(k):
        return remote(own_tok, own_tok, TY, ty_r.at[k - 1], at_y(k))

    def tok_f(k, n):
        here = T.at[(y + NY - k) % NY, pl.ds(x * 4, 4)]
        return remote(here, here, TF, tf_r.at[k - 1], at_x(n))

    three = T.at[0, pl.ds(0, 12)]

    for k in (2, 1, 3):
        tok_x(k).start()
    for k in (1, 3, 2):
        tok_y(k).start()

    @pl.loop(1, N)
    def _(j):
        for q in range(NY):
            w_copy(j, q).start()

    cot_copy.wait()
    arrived(three, tx_r.at[0])

    def pc(j):
        return remote(Pb.at[j, 1 - c], Rc.at[j], PC, pc_r.at[j], other)

    SUMS = ((4, -2, 0), (-3, -1, 1), (3, 1, 2), (-1, -1, 3), (1, 1, 4), (-2, -2, 5), (2, 2, 6))

    def rs(j, n):
        owner, to, place = SUMS[n]
        here, recv = (R1.at[j, place], ra_r) if place < 3 else (R2.at[j, place - 3], rb_r)
        return remote(SB.at[j, zmod(owner * d)], here, RS, recv.at[j], at_z(to * d))

    def yt(j, k):
        return remote(GS.at[j, (y + k) % NY], G.at[j, y, z, c], YT, yt_r.at[j], at_y(k))

    AG = ((0, 1), (0, -1), (0, 2), (0, -2), (-2, 1), (-2, 2), (2, -1))

    def ag(j, n):
        origin, to = AG[n]
        piece = G.at[j, :, zmod(origin * d), c]
        recv = ag_r.at[j, {2: 0, 3: 1}.get(n, 2)]
        return remote(piece, piece, AGS, recv, at_z(to * d))

    def gc(j):
        piece = G.at[j, :, :, c]
        return remote(piece, piece, GC, gc_r.at[j], other)

    def out_columns(group, j):
        return out.at[:, pl.ds(pl.multiple_of(group * QUARTER + j * CW, CW), CW)]

    def wo(j, k):
        return remote(WG.at[j, k], out_columns(y, j), WO, wo_r.at[0], at_y(k))

    def wo_own(j):
        return pltpu.make_async_copy(WG.at[j, 0], out_columns(y, j), o_sem.at[0])

    def project(j):
        slot = j % 3
        rows = T[y].reshape(NZ * 2 * ROWS, KD)
        pltpu.make_async_copy(Wv.at[j], Wv.at[j], w_sem.at[j]).wait()
        for q in range(NY):
            part = jnp.dot(rows, Wv[j, q], preferred_element_type=F32)
            part = part.reshape(NZ, 2, ROWS, CW)
            for core in range(2):
                Pf[slot, core, :, q] = part[:, core]
                Pb[j, core, :, q] = part[:, core].astype(BF16)
        pc(j).start()

    def reduce_first(j):
        arrived(Rc.at[j], pc_r.at[j])
        both = Pf[j % 3, c] + Rc[j].astype(F32)
        S32[j] = both
        SB[j] = both.astype(BF16)
        for n in (0, 1, 2, 3, 4):
            rs(j, n).start()

    def reduce_second(j):
        arrived(R1.at[j], ra_r.at[j])
        near, far = zmod(-2 * d), zmod(2 * d)
        SB[j, near] = (S32[j, near] + R1[j, 0].astype(F32) + R1[j, 1].astype(F32)).astype(BF16)
        rs(j, 5).start()
        SB[j, far] = (S32[j, far] + R1[j, 2].astype(F32)).astype(BF16)
        rs(j, 6).start()

    def activate(j):
        arrived(R2.at[j], rb_r.at[j])
        v = S32[j, z] + R2[j, 0].astype(F32) + R2[j, 1].astype(F32)
        v = v + R2[j, 2].astype(F32) + R2[j, 3].astype(F32)
        square = v * v
        t = jnp.tanh(C1 * (v + C2 * (v * square)))
        half = 0.5 * (1.0 + t)
        slope = half + 0.5 * v * (1.0 - t * t) * (C1 * (1.0 + 3.0 * C2 * square))
        hidden = (v * half).astype(BF16)
        for q in range(NY):
            columns = pl.ds(pl.multiple_of(q * QUARTER + j * CW, CW), CW)
            H[:, columns] = hidden[q]
            GS[j, q] = (C[:, columns].astype(F32) * slope[q]).astype(BF16)
        for k in (2, 1, 3):
            yt(j, k).start()
        G[j, y, z, c] = GS[j, y]

    def gather_first(j):
        arrived(GS.at[j, pl.ds(0, 3)], yt_r.at[j])
        for n in (2, 3, 0, 1):
            ag(j, n).start()

    def gather_second(j):
        arrived(SB.at[j, 0], ag_r.at[j, 0])
        ag(j, 5).start()
        ag(j, 4).start()
        arrived(SB.at[j, 0], ag_r.at[j, 1])
        ag(j, 6).start()

    def gather_cores(j):
        arrived(SB.at[j, pl.ds(0, 5)], ag_r.at[j, 2])
        gc(j).start()

    def weight_product(j):
        arrived(G.at[j, :, :, 1 - c], gc_r.at[j])
        for k in (2, 1, 3, 0):
            grad = G[j].reshape(NY * NZ * 2 * ROWS, CW)
            WG[j, k] = jnp.dot(TT[(y + k) % NY], grad, preferred_element_type=F32).astype(BF16)
            if k:
                wo(j, k).start()
            else:
                wo_own(j).start()

    def forward(t):
        for k in (1, 3, 2):
            arrived(own_tok, ty_r.at[k - 1])
            for n in (2, 1, 3):
                tok_f(k, n).start()

    def turn(t):
        def run(k):
            if k:
                arrived(three, tf_r.at[k - 1])
            group = (y + NY - k) % NY
            turned = T[group].reshape(NZ * 2 * ROWS, KD).T.reshape(NY, OWN, NZ * 2 * ROWS)
            TT[:, :, pl.ds(pl.multiple_of(group * 256, 256), 256)] = turned

        for k in range(NY):
            pl.when(t == TURN[k])(lambda k=k: run(k))

    stages = {
        "project": project, "reduce_first": reduce_first, "reduce_second": reduce_second,
        "activate": activate, "gather_first": gather_first, "gather_second": gather_second,
        "gather_cores": gather_cores, "weight_product": weight_product,
    }

    @pl.loop(min(AT.values()), N + AT["weight_product"])
    def _(t):
        for name in ORDER:
            if name == "forward":
                pl.when(t == FORWARD)(lambda: forward(t))
            elif name == "turn":
                turn(t)
            else:
                j = t - AT[name]
                pl.when(jnp.logical_and(j >= 0, j < N))(lambda run=stages[name], j=j: run(j))

    hid_copy = pltpu.make_async_copy(H, hid, l_sem.at[2])
    hid_copy.start()
    sent(three, TX)
    sent(three, TY)
    sent(T.at[pl.ds(0, 3), pl.ds(0, 12)], TF)
    sent(Pb.at[:, 0], PC)
    sent(SB.at[:, pl.ds(0, 7)], RS)
    sent(GS.at[:, pl.ds(0, 3)], YT)
    sent(SB.at[:, pl.ds(0, 7)], AGS)
    sent(G.at[:, :, :, 0], GC)
    sent(WG.at[:, pl.ds(0, 3)], WO)
    arrived(WG.at[:, pl.ds(0, 3)], wo_r.at[0])
    pltpu.make_async_copy(WG.at[:, 0], WG.at[:, 0], o_sem.at[0]).wait()
    hid_copy.wait()


def place(hidden, grad, hidden_out, grad_out, sems):
    copies = [pltpu.make_async_copy(hidden, hidden_out, sems.at[0])]
    for n in range(4):
        rows = pl.ds(n * 48, 48)
        copies.append(pltpu.make_async_copy(grad.at[rows], grad_out.at[rows], sems.at[1 + n]))
    for copy in copies:
        copy.start()
    for copy in copies:
        copy.wait()


def local(tokens, weight, cotangent):
    dma = pltpu.SemaphoreType.DMA
    piece = (NY, ROWS, CW)
    any_ref = pl.BlockSpec(memory_space=pl.ANY)
    hidden, grad = pl.pallas_call(
        kernel,
        out_shape=[
            jax.ShapeDtypeStruct(cotangent.shape, BF16),
            jax.ShapeDtypeStruct((OWN, weight.shape[1]), BF16),
        ],
        in_specs=[pl.BlockSpec(memory_space=pltpu.HBM)] * 3,
        out_specs=[any_ref] * 2,
        scratch_shapes=[
            pltpu.VMEM((NY, NZ * 2, ROWS, KD), BF16),
            pltpu.VMEM((NY, OWN, 1024), BF16),
            pltpu.VMEM((N, NY, KD, CW), BF16),
            pltpu.VMEM((3, 2, NZ) + piece, F32),
            pltpu.VMEM((N, 2, NZ) + piece, BF16),
            pltpu.VMEM((N, NZ) + piece, BF16),
            pltpu.VMEM((N, NZ) + piece, F32),
            pltpu.VMEM((N, NZ) + piece, BF16),
            pltpu.VMEM((N, 3) + piece, BF16),
            pltpu.VMEM((N, 4) + piece, BF16),
            pltpu.VMEM((N, NY, NZ, 2, ROWS, CW), BF16),
            pltpu.VMEM((N,) + piece, BF16),
            pltpu.VMEM(cotangent.shape, BF16),
            pltpu.VMEM(cotangent.shape, BF16),
            pltpu.VMEM((N, NY, OWN, CW), BF16),
            dma((9,)), dma((1,)), dma((3,)), dma((3,)), dma((N,)), dma((N,)), dma((N,)), dma((N,)),
            dma((N, 3)), dma((N,)), dma((1,)), dma((N,)), dma((3,)), dma((1,)),
        ],
        compiler_params=pltpu.CompilerParams(
            collective_id=0, has_side_effects=True, vmem_limit_bytes=51 * 2**20
        ),
        cost_estimate=pl.CostEstimate(
            flops=4 * 256 * 768 * 6144, bytes_accessed=13 * 2**20, transcendentals=16 * 6144
        ),
    )(*[pltpu.with_memory_space_constraint(a, pltpu.HBM) for a in (tokens.reshape(4, ROWS, KD), weight, cotangent)])
    return pl.pallas_call(
        place,
        out_shape=[jax.ShapeDtypeStruct(a.shape, BF16) for a in (hidden, grad)],
        in_specs=[any_ref] * 2,
        out_specs=[any_ref] * 2,
        scratch_shapes=[dma((5,))],
    )(*[pltpu.with_memory_space_constraint(a, pltpu.VMEM) for a in (hidden, grad)])


def solution(mesh):
    return jax.shard_map(
        local,
        mesh=mesh,
        in_specs=(P(("dp", "depth"), "grid"), P("grid", "depth"), P(("dp", "grid"), "depth")),
        out_specs=(P(("dp", "grid"), "depth"), P(("grid", "dp"), "depth")),
        check_vma=False,
    )
```

```python
import jax
import jax.numpy as jnp
from jax import lax
from jax.experimental import pallas as pl
from jax.experimental.pallas import tpu as pltpu
from jax.sharding import PartitionSpec as P

MESH = pl.DeviceIdType.MESH
F32, BF16 = jnp.float32, jnp.bfloat16
NY, NX, NZ = 4, 4, 8
N = 12
CW = 128
AT = {"project": -5, "reduce_first": -4, "reduce_second": -1, "activate": 2, "gather_first": 4, "gather_second": 6, "gather_cores": 7, "weight_product": 8}
ORDER = ["activate", "turn", "forward", "gather_second", "gather_first", "reduce_second", "weight_product", "project", "gather_cores", "reduce_first"]
FORWARD = -3
TURN = (0, 2, 5, 6)
QUARTER = N * CW
KD = 768
ROWS = 16
OWN = 192
C1 = 0.7978845608028654
C2 = 0.044715


TX, TY, TF, PC, RS, YT, AGS, GC, WO = range(9)


def kernel(
    tok, wt, cot, hid, out,
    T, TT, Wv, Pf, Pb, Rc, S32, SB, R1, R2, G, GS, C, H, WG,
    send, tx_r, ty_r, tf_r, pc_r, ra_r, rb_r, yt_r, ag_r, gc_r, wo_r, w_sem, l_sem, o_sem,
):
    y, x, g = lax.axis_index("dp"), lax.axis_index("depth"), lax.axis_index("grid")
    z, c = g // 2, g % 2
    d = 1 - 2 * c

    def zmod(k):
        return (z + k + NZ) % NZ

    def at_z(k):
        return (y, x, zmod(k) * 2 + c)

    def at_x(k):
        return (y, (x + k) % NX, g)

    def at_y(k):
        return ((y + k) % NY, x, g)

    other = (y, x, z * 2 + 1 - c)

    def remote(src, dst, kind, recv, device):
        return pltpu.make_async_remote_copy(
            src_ref=src, dst_ref=dst, send_sem=send.at[kind], recv_sem=recv,
            device_id=device, device_id_type=MESH,
        )

    def arrived(like, recv):
        remote(like, like, 0, recv, other).wait_recv()

    def sent(like, kind):
        remote(like, like, kind, tx_r.at[0], other).wait_send()

    barrier = pltpu.get_barrier_semaphore()
    peers = [at_x(2), at_y(2), at_z(2), at_z(-2), at_x(1), at_x(3), at_y(1), at_y(3), at_z(1), at_z(-1), other]
    for peer in peers:
        pl.semaphore_signal(barrier, inc=1, device_id=peer, device_id_type=MESH)

    own_tok = T.at[y, pl.ds(x * 4, 4)]
    tok_copy = pltpu.make_async_copy(tok, own_tok, l_sem.at[0])
    tok_copy.start()

    def w_copy(j, q):
        columns = pl.ds(pl.multiple_of(q * QUARTER + j * CW, CW), CW)
        return pltpu.make_async_copy(wt.at[:, columns], Wv.at[j, q], w_sem.at[j])

    for q in range(NY):
        w_copy(0, q).start()
    cot_copy = pltpu.make_async_copy(cot, C, l_sem.at[1])
    cot_copy.start()

    tok_copy.wait()
    pl.semaphore_wait(barrier, len(peers))

    def tok_x(k):
        return remote(own_tok, own_tok, TX, tx_r.at[0], at_x(k))

    def tok_y(k):
        return remote(own_tok, own_tok, TY, ty_r.at[k - 1], at_y(k))

    def tok_f(k, n):
        here = T.at[(y + NY - k) % NY, pl.ds(x * 4, 4)]
        return remote(here, here, TF, tf_r.at[k - 1], at_x(n))

    three = T.at[0, pl.ds(0, 12)]

    for k in (2, 1, 3):
        tok_x(k).start()
    for k in (1, 3, 2):
        tok_y(k).start()

    @pl.loop(1, N)
    def _(j):
        for q in range(NY):
            w_copy(j, q).start()

    cot_copy.wait()
    arrived(three, tx_r.at[0])

    def pc(j):
        return remote(Pb.at[j, 1 - c], Rc.at[j], PC, pc_r.at[j], other)

    SUMS = ((4, -2, 0), (-3, -1, 1), (3, 1, 2), (-1, -1, 3), (1, 1, 4), (-2, -2, 5), (2, 2, 6))

    def rs(j, n):
        owner, to, place = SUMS[n]
        here, recv = (R1.at[j, place], ra_r) if place < 3 else (R2.at[j, place - 3], rb_r)
        return remote(SB.at[j, zmod(owner * d)], here, RS, recv.at[j], at_z(to * d))

    def yt(j, k):
        return remote(GS.at[j, (y + k) % NY], G.at[j, y, z, c], YT, yt_r.at[j], at_y(k))

    AG = ((0, 1), (0, -1), (0, 2), (0, -2), (-2, 1), (-2, 2), (2, -1))

    def ag(j, n):
        origin, to = AG[n]
        piece = G.at[j, :, zmod(origin * d), c]
        recv = ag_r.at[j, {2: 0, 3: 1}.get(n, 2)]
        return remote(piece, piece, AGS, recv, at_z(to * d))

    def gc(j):
        piece = G.at[j, :, :, c]
        return remote(piece, piece, GC, gc_r.at[j], other)

    def out_columns(group, j):
        return out.at[:, pl.ds(pl.multiple_of(group * QUARTER + j * CW, CW), CW)]

    def wo(j, k):
        return remote(WG.at[j, k], out_columns(y, j), WO, wo_r.at[0], at_y(k))

    def wo_own(j):
        return pltpu.make_async_copy(WG.at[j, 0], out_columns(y, j), o_sem.at[0])

    def project(j):
        slot = j % 3
        rows = T[y].reshape(NZ * 2 * ROWS, KD)
        pltpu.make_async_copy(Wv.at[j], Wv.at[j], w_sem.at[j]).wait()
        for q in range(NY):
            part = jnp.dot(rows, Wv[j, q], preferred_element_type=F32)
            part = part.reshape(NZ, 2, ROWS, CW)
            for core in range(2):
                Pf[slot, core, :, q] = part[:, core]
                Pb[j, core, :, q] = part[:, core].astype(BF16)
        pc(j).start()

    def reduce_first(j):
        arrived(Rc.at[j], pc_r.at[j])
        both = Pf[j % 3, c] + Rc[j].astype(F32)
        S32[j] = both
        SB[j] = both.astype(BF16)
        for n in (0, 1, 2, 3, 4):
            rs(j, n).start()

    def reduce_second(j):
        arrived(R1.at[j], ra_r.at[j])
        near, far = zmod(-2 * d), zmod(2 * d)
        SB[j, near] = (S32[j, near] + R1[j, 0].astype(F32) + R1[j, 1].astype(F32)).astype(BF16)
        rs(j, 5).start()
        SB[j, far] = (S32[j, far] + R1[j, 2].astype(F32)).astype(BF16)
        rs(j, 6).start()

    def activate(j):
        arrived(R2.at[j], rb_r.at[j])
        v = S32[j, z] + R2[j, 0].astype(F32) + R2[j, 1].astype(F32)
        v = v + R2[j, 2].astype(F32) + R2[j, 3].astype(F32)
        square = v * v
        t = jnp.tanh(C1 * (v + C2 * (v * square)))
        half = 0.5 * (1.0 + t)
        slope = half + 0.5 * v * (1.0 - t * t) * (C1 * (1.0 + 3.0 * C2 * square))
        hidden = (v * half).astype(BF16)
        for q in range(NY):
            columns = pl.ds(pl.multiple_of(q * QUARTER + j * CW, CW), CW)
            H[:, columns] = hidden[q]
            GS[j, q] = (C[:, columns].astype(F32) * slope[q]).astype(BF16)
        for k in (2, 1, 3):
            yt(j, k).start()
        G[j, y, z, c] = GS[j, y]

    def gather_first(j):
        arrived(GS.at[j, pl.ds(0, 3)], yt_r.at[j])
        for n in (2, 3):
            ag(j, n).start()

    def gather_second(j):
        arrived(SB.at[j, 0], ag_r.at[j, 0])
        ag(j, 5).start()
        ag(j, 4).start()
        arrived(SB.at[j, 0], ag_r.at[j, 1])
        ag(j, 6).start()
        ag(j, 0).start()
        ag(j, 1).start()

    def gather_cores(j):
        arrived(SB.at[j, pl.ds(0, 5)], ag_r.at[j, 2])
        gc(j).start()

    def weight_product(j):
        arrived(G.at[j, :, :, 1 - c], gc_r.at[j])
        for k in (2, 1, 3, 0):
            grad = G[j].reshape(NY * NZ * 2 * ROWS, CW)
            WG[j, k] = jnp.dot(TT[(y + k) % NY], grad, preferred_element_type=F32).astype(BF16)
            if k:
                wo(j, k).start()
            else:
                wo_own(j).start()

    def forward(t):
        for k in (1, 3, 2):
            arrived(own_tok, ty_r.at[k - 1])
            for n in (2, 1, 3):
                tok_f(k, n).start()

    def turn(t):
        def run(k):
            if k:
                arrived(three, tf_r.at[k - 1])
            group = (y + NY - k) % NY
            turned = T[group].reshape(NZ * 2 * ROWS, KD).T.reshape(NY, OWN, NZ * 2 * ROWS)
            TT[:, :, pl.ds(pl.multiple_of(group * 256, 256), 256)] = turned

        for k in range(NY):
            pl.when(t == TURN[k])(lambda k=k: run(k))

    stages = {
        "project": project, "reduce_first": reduce_first, "reduce_second": reduce_second,
        "activate": activate, "gather_first": gather_first, "gather_second": gather_second,
        "gather_cores": gather_cores, "weight_product": weight_product,
    }

    @pl.loop(min(AT.values()), N + AT["weight_product"])
    def _(t):
        for name in ORDER:
            if name == "forward":
                pl.when(t == FORWARD)(lambda: forward(t))
            elif name == "turn":
                turn(t)
            else:
                j = t - AT[name]
                pl.when(jnp.logical_and(j >= 0, j < N))(lambda run=stages[name], j=j: run(j))

    hid_copy = pltpu.make_async_copy(H, hid, l_sem.at[2])
    hid_copy.start()
    sent(three, TX)
    sent(three, TY)
    sent(T.at[pl.ds(0, 3), pl.ds(0, 12)], TF)
    sent(Pb.at[:, 0], PC)
    sent(SB.at[:, pl.ds(0, 7)], RS)
    sent(GS.at[:, pl.ds(0, 3)], YT)
    sent(SB.at[:, pl.ds(0, 7)], AGS)
    sent(G.at[:, :, :, 0], GC)
    sent(WG.at[:, pl.ds(0, 3)], WO)
    arrived(WG.at[:, pl.ds(0, 3)], wo_r.at[0])
    pltpu.make_async_copy(WG.at[:, 0], WG.at[:, 0], o_sem.at[0]).wait()
    hid_copy.wait()


def place(hidden, grad, hidden_out, grad_out, sems):
    copies = [pltpu.make_async_copy(hidden, hidden_out, sems.at[0])]
    for n in range(4):
        rows = pl.ds(n * 48, 48)
        copies.append(pltpu.make_async_copy(grad.at[rows], grad_out.at[rows], sems.at[1 + n]))
    for copy in copies:
        copy.start()
    for copy in copies:
        copy.wait()


def local(tokens, weight, cotangent):
    dma = pltpu.SemaphoreType.DMA
    piece = (NY, ROWS, CW)
    any_ref = pl.BlockSpec(memory_space=pl.ANY)
    hidden, grad = pl.pallas_call(
        kernel,
        out_shape=[
            jax.ShapeDtypeStruct(cotangent.shape, BF16),
            jax.ShapeDtypeStruct((OWN, weight.shape[1]), BF16),
        ],
        in_specs=[pl.BlockSpec(memory_space=pltpu.HBM)] * 3,
        out_specs=[any_ref] * 2,
        scratch_shapes=[
            pltpu.VMEM((NY, NZ * 2, ROWS, KD), BF16),
            pltpu.VMEM((NY, OWN, 1024), BF16),
            pltpu.VMEM((N, NY, KD, CW), BF16),
            pltpu.VMEM((3, 2, NZ) + piece, F32),
            pltpu.VMEM((N, 2, NZ) + piece, BF16),
            pltpu.VMEM((N, NZ) + piece, BF16),
            pltpu.VMEM((N, NZ) + piece, F32),
            pltpu.VMEM((N, NZ) + piece, BF16),
            pltpu.VMEM((N, 3) + piece, BF16),
            pltpu.VMEM((N, 4) + piece, BF16),
            pltpu.VMEM((N, NY, NZ, 2, ROWS, CW), BF16),
            pltpu.VMEM((N,) + piece, BF16),
            pltpu.VMEM(cotangent.shape, BF16),
            pltpu.VMEM(cotangent.shape, BF16),
            pltpu.VMEM((N, NY, OWN, CW), BF16),
            dma((9,)), dma((1,)), dma((3,)), dma((3,)), dma((N,)), dma((N,)), dma((N,)), dma((N,)),
            dma((N, 3)), dma((N,)), dma((1,)), dma((N,)), dma((3,)), dma((1,)),
        ],
        compiler_params=pltpu.CompilerParams(
            collective_id=0, has_side_effects=True, vmem_limit_bytes=51 * 2**20
        ),
        cost_estimate=pl.CostEstimate(
            flops=4 * 256 * 768 * 6144, bytes_accessed=13 * 2**20, transcendentals=16 * 6144
        ),
    )(*[pltpu.with_memory_space_constraint(a, pltpu.HBM) for a in (tokens.reshape(4, ROWS, KD), weight, cotangent)])
    return pl.pallas_call(
        place,
        out_shape=[jax.ShapeDtypeStruct(a.shape, BF16) for a in (hidden, grad)],
        in_specs=[any_ref] * 2,
        out_specs=[any_ref] * 2,
        scratch_shapes=[dma((5,))],
    )(*[pltpu.with_memory_space_constraint(a, pltpu.VMEM) for a in (hidden, grad)])


def solution(mesh):
    return jax.shard_map(
        local,
        mesh=mesh,
        in_specs=(P(("dp", "depth"), "grid"), P("grid", "depth"), P(("dp", "grid"), "depth")),
        out_specs=(P(("dp", "grid"), "depth"), P(("grid", "dp"), "depth")),
        check_vma=False,
    )
```
